256 devices in a mesh: dp: 64 (over x, y, z_lo), grp: 4 (over z_hi, core).
Axes of the slice: x: 4, y: 4, z: 8 (z_hi: 2, z_lo: 4; z = z_hi * 4 + z_lo), core: 2. Of those that a mesh axis runs over, the one named last changes fastest.
Arguments:
- acts: bfloat16 [32768, 5120], P(('dp', 'grp')), may hold values from -6 to 6
- grads: bfloat16 [32768, 5120], P(('dp', 'grp')), may hold values from -6 to 6
- basis_a: bfloat16 [8, 640, 640], P(None, 'grp'), may hold values from -0.25 to 0.25
- basis_g: bfloat16 [8, 640, 640], P(None, 'grp'), may hold values from -0.25 to 0.25
- eig_a: float32 [8, 640], replicated, may hold values from 0.3 to 3
- eig_g: float32 [8, 640], replicated, may hold values from 0.3 to 3
Outputs:
- factor_a: float32 [5120, 640], P(('dp', 'grp'))
- factor_g: float32 [5120, 640], P(('dp', 'grp'))
- precond: bfloat16 [64, 640, 640], P('dp', None, 'grp')
The draws below stay inside these ranges and needn't reach their ends.
All inputs are finite; a program needn't handle non-finite values.
Results may differ from the reference program's by a relative error of at most 0.022.
Values may be sent and summed in bfloat16 or wider, within the bound.
No kernel may reach another device: no remote copies, remote signals or barrier semaphores. Data moves between devices by JAX's collectives and lax.ppermute only.
A program may use at most 128 MiB of HBM per device.

```python
import math
import jax
import jax.numpy as jnp
from jax import lax

D = 5120
BLK = 640
TOK_DEV = 128
NB = 8
TOKENS = 32768


def block_scale(own_key, dims, split, least, top_value):
    factor_of = 1.0
    for axis_at, blocks in split:
        draws = jax.random.uniform(jax.random.fold_in(jax.random.fold_in(own_key, 6), axis_at), (blocks,), jnp.float32, least / len(split), top_value / len(split))
        factor_of = factor_of * jnp.repeat(jnp.exp(draws), dims[axis_at] // blocks).reshape((-1,) + (1,) * (len(dims) - 1 - axis_at))
    return factor_of


def noise(rng, dims, deviation, bound, split=(), kind=jnp.bfloat16):
    array = jax.random.normal(rng, dims, jnp.float32) * deviation
    if len(split) > 0:
        array = block_scale(rng, dims, split, -0.22, 0.18) * array
    return jnp.clip(array, min=-bound, max=bound).astype(kind)


def setup_inputs(seed: int = 0) -> dict:
    streams_of = jax.random.split(jax.random.key(seed), 7)
    return {
        "acts": noise(streams_of[0], (TOKENS, D), 1.0, 6.0, ((0, 256),)),
        "grads": noise(streams_of[1], (TOKENS, D), 1.0, 6.0, ((0, 256),)),
        "basis_a": noise(streams_of[2], (NB, BLK, BLK), BLK ** -0.5, 0.25, ((1, 4),)),
        "basis_g": noise(streams_of[3], (NB, BLK, BLK), BLK ** -0.5, 0.25, ((1, 4),)),
        "eig_a": jnp.clip(jnp.exp(jax.random.uniform(streams_of[4], (NB, BLK), jnp.float32, math.log(0.3), math.log(3.0))), 0.3, 3.0),
        "eig_g": jnp.clip(jnp.exp(jax.random.uniform(streams_of[5], (NB, BLK), jnp.float32, math.log(0.3), math.log(3.0))), 0.3, 3.0),
    }


damping = 0.03


def rotate_tile(basis_left, basis_right, tile, eig_left, eig_right):
    left = jnp.dot(basis_left.T, tile, preferred_element_type=jnp.float32).astype(jnp.bfloat16)
    rotated = jnp.dot(left, basis_right, preferred_element_type=jnp.float32)
    scaled = (rotated / (eig_left[:, None] * eig_right[None, :] + damping)).astype(jnp.bfloat16)
    right = jnp.dot(scaled, basis_right.T, preferred_element_type=jnp.float32).astype(jnp.bfloat16)
    return jnp.dot(basis_left, right, preferred_element_type=jnp.float32).astype(jnp.bfloat16)


def reference(acts, grads, basis_a, basis_g, eig_a, eig_g):
    acts_full = acts.astype(jnp.float32)
    grads_full = grads.astype(jnp.float32)
    acts_blocks = acts_full.reshape(TOKENS, NB, BLK)
    grads_blocks = grads_full.reshape(TOKENS, NB, BLK)
    blocks_a = jnp.einsum('tbi,tbj->bij', acts_blocks, acts_blocks) / TOKENS
    blocks_g = jnp.einsum('tbi,tbj->bij', grads_blocks, grads_blocks) / TOKENS
    factor_a = blocks_a.reshape(D, BLK)
    factor_g = blocks_g.reshape(NB, NB, BLK // NB, BLK).transpose(1, 0, 2, 3).reshape(D, BLK)
    wgrad = jnp.einsum('ti,tj->ij', acts_full, grads_full) / TOK_DEV
    tiles = wgrad.astype(jnp.bfloat16).reshape(NB, BLK, NB, BLK).transpose(0, 2, 1, 3).reshape(NB * NB, BLK, BLK)
    numbers = jnp.arange(NB * NB, dtype=jnp.int32)

    def one_tile(item):
        number, tile = item
        row_block = number // NB
        col_block = number % NB
        return rotate_tile(basis_a[row_block], basis_g[col_block], tile, eig_a[row_block], eig_g[col_block])

    precond = lax.map(one_tile, (numbers, tiles))
    return factor_a, factor_g, precond
```

```python
import jax
import jax.numpy as jnp
from jax import lax
from jax.experimental import pallas as pl
from jax.experimental.pallas import tpu as pltpu
from jax.sharding import Mesh, PartitionSpec as P

DAMPING = 0.03
ROWS = (((0,), (0,)), ((), ()))
COLS = (((1,), (1,)), ((), ()))
MIB = 1 << 20
F32 = jnp.float32
BF16 = jnp.bfloat16
VMEM = pl.BlockSpec(memory_space=pltpu.VMEM)
SMEM = pl.BlockSpec(memory_space=pltpu.SMEM)
PLACE = (0, 4, 1, 5, 3, 7, 2, 6)


def shift(count, by):
    return [(i, (i + by) % count) for i in range(count)]


def z_shift(by):
    at = [(z % 4) * 2 + z // 4 for z in range(8)]
    return [(at[z], at[(z + by) % 8]) for z in range(8)]


def to_z(array, by):
    return lax.ppermute(array, ("zl", "zh"), z_shift(by))


def swap(array, axis="core"):
    return lax.ppermute(array, axis, shift(2, 1))


def params(mib=50):
    return pltpu.CompilerParams(vmem_limit_bytes=mib * MIB)


def exchange(array, axis, count, width):
    me = lax.axis_index(axis)
    pieces = []
    for d in range(count):
        block = lax.dynamic_slice_in_dim(array, lax.rem(me + d, count) * width, width, 1)
        pieces.append(block if d == 0 else lax.ppermute(block, axis, shift(count, d)))
    return jnp.concatenate(pieces, axis=0)


def gather_near(own, axis):
    return own, lax.ppermute(own, axis, shift(4, 1)), lax.ppermute(own, axis, shift(4, 3))


def gather_far(near, axis):
    _, back, ahead = near
    half = back.shape[0] // 2
    return (
        lax.ppermute(back[:half], axis, shift(4, 1)),
        lax.ppermute(ahead[half:], axis, shift(4, 3)),
    )


def rows_of(near, far, d, e, cols):
    if d == 2:
        ref, at = far[e // 2], e % 2
    else:
        ref, at = near[(0, 1, None, 2)[d]], e
    return ref[at * 128 : (at + 1) * 128, cols]


def tokens(near, far, pairs, cols):
    return jnp.concatenate([rows_of(near, far, d, e, cols) for d, e in pairs], axis=0)


def product(left_rows, right_rows, groups):
    total = None
    for group in groups:
        part = lax.dot_general(
            left_rows(group), right_rows(group), ROWS, preferred_element_type=F32
        )
        total = part if total is None else total + part
    return total


def flipped(group):
    return [(e, d) for d, e in group]


NEAR = [[(d, e) for d in (0, 1, 3)] for e in (0, 1, 3)]
FAR = [[(d, 2) for d in range(4)], [(2, e) for e in (0, 1, 3)]]


def block(i):
    return slice(i * 640, i * 640 + 640)


def near_kernel(*refs):
    acts, grads, total_ref = refs[:3], refs[3:6], refs[6]
    for b in range(2):
        for c in range(2):
            total_ref[b, c] = product(
                lambda g: tokens(grads, None, g, block(c)),
                lambda g: tokens(acts, None, flipped(g), block(b)),
                NEAR,
            )


def far_kernel(where_ref, *refs):
    acts, grads, acts_far, grads_far = refs[:3], refs[3:6], refs[6:8], refs[8:10]
    total_ref, keep_ref, send_ref = refs[10:]
    z, core = where_ref[0], where_ref[1]
    for b in range(2):
        for c in range(2):
            total = total_ref[b, c] + product(
                lambda g: tokens(grads, grads_far, g, block(c)),
                lambda g: tokens(acts, acts_far, flipped(g), block(b)),
                FAR,
            )
            for q in range(4):
                away = lax.rem(4 * b + 2 * c + q // 2 - z + 8, 8)
                place = 0
                for d in range(8):
                    place = jnp.where(away == d, PLACE[d], place)
                piece = total[q * 160 : q * 160 + 160]

                @pl.when(core == q % 2)
                def _():
                    keep_ref[place] = piece

                @pl.when(core != q % 2)
                def _():
                    send_ref[place] = piece


def factor_kernel(where_ref, *refs):
    acts, grads, acts_far, grads_far = refs[:3], refs[3:6], refs[6:8], refs[8:10]
    fa_ref, fg_ref = refs[10:]
    y, x = where_ref[0], where_ref[1]
    groups = [[(d, e) for d in range(4)] for e in range(4)]
    base = pl.multiple_of((y // 2) * 640, 128)
    window = pl.multiple_of((y // 2) * 640 + (y % 2) * 256, 128)
    fa_ref[...] = product(
        lambda g: tokens(acts, acts_far, g, pl.ds(window, 384)),
        lambda g: tokens(acts, acts_far, g, pl.ds(base, 640)),
        groups,
    )
    for c in range(2):
        window = pl.multiple_of(c * 640 + x * 128, 128)
        fg_ref[c] = product(
            lambda g: tokens(grads, grads_far, g, pl.ds(window, 256)),
            lambda g: tokens(grads, grads_far, g, block(c)),
            groups,
        )


def left_kernel(p0, p1, p2, p3, p4, p5, qa_ref, left_ref):
    total = p0[...].astype(F32)
    for p in (p1, p2, p3, p4, p5):
        total += p[...].astype(F32)
    wgrad = (total / 128).astype(BF16)
    qa = qa_ref[...].reshape(640, 640)
    left_ref[...] = jnp.dot(wgrad, qa, preferred_element_type=F32).astype(BF16)


def finish_kernel(l0, l1, l2, l3, qg_ref, qa_ref, eig_a_ref, eig_g_ref, out_ref):
    rotated = None
    for r, left in enumerate((l0, l1, l2, l3)):
        part = lax.dot_general(qg_ref[r], left[...], ROWS, preferred_element_type=F32)
        rotated = part if rotated is None else rotated + part
    scaled = (rotated / (eig_g_ref[...] * eig_a_ref[...] + DAMPING)).astype(BF16)
    right = jnp.dot(qg_ref[0], scaled, preferred_element_type=F32).astype(BF16)
    out_ref[...] = lax.dot_general(
        qa_ref[...].reshape(640, 640), right, COLS, preferred_element_type=F32
    ).astype(BF16)


def sum_over_z(own):
    prev = to_z(own[4:6], 1)
    after = to_z(own[6:8], 7)
    opposite = to_z(own[3], 4)
    ahead = (own[1].astype(F32) + prev[1].astype(F32)).astype(BF16)
    behind = (own[2].astype(F32) + after[1].astype(F32)).astype(BF16)
    ahead, behind = to_z(ahead, 2), to_z(behind, 6)
    return own[0], prev[0], after[0], opposite, ahead, behind


def body(acts, grads, basis_a, basis_g, eig_a, eig_g):
    x, y, zl, zh, core = (lax.axis_index(n) for n in ("x", "y", "zl", "zh", "core"))
    z = 4 * zh + zl
    block_a, block_g = 2 * x + zh, 2 * y + zl // 2
    quarter = 2 * (zl % 2) + core

    def basis_pair(i):
        return jnp.stack(
            [
                lax.dynamic_index_in_dim(basis_a, i, 0, keepdims=False),
                lax.dynamic_index_in_dim(basis_g, block_g, 0, keepdims=False),
            ]
        )

    basis_far = swap(basis_pair(2 * x + 1 - zh), "zh")
    acts_x = exchange(acts, "x", 4, 1280)
    grads_y = exchange(grads, "y", 4, 1280)
    acts_x, grads_y, basis_far = lax.optimization_barrier((acts_x, grads_y, basis_far))
    here = jnp.stack([basis_pair(block_a), basis_far])
    sibling = swap(here)
    acts_near = gather_near(acts_x, "y")
    grads_near = gather_near(grads_y, "x")
    acts_far = gather_far(acts_near, "y")
    grads_far = gather_far(grads_near, "x")

    total = pl.pallas_call(
        near_kernel,
        out_shape=jax.ShapeDtypeStruct((2, 2, 640, 640), F32),
        in_specs=[VMEM] * 6,
        out_specs=VMEM,
        compiler_params=params(),
        cost_estimate=pl.CostEstimate(flops=4 * 10**9, bytes_accessed=10**7, transcendentals=0),
    )(*acts_near, *grads_near)
    operands = (*acts_near, *grads_near, *acts_far, *grads_far)
    w_keep, w_send = pl.pallas_call(
        far_kernel,
        out_shape=(jax.ShapeDtypeStruct((8, 160, 640), F32),) * 2,
        in_specs=[SMEM] + [VMEM] * 11,
        out_specs=(VMEM, VMEM),
        compiler_params=params(),
        cost_estimate=pl.CostEstimate(flops=3 * 10**9, bytes_accessed=10**7, transcendentals=0),
    )(jnp.stack([z, core]).astype(jnp.int32), *operands, total)

    by_core = jnp.where(core == 0, jnp.stack([here, sibling], 1), jnp.stack([sibling, here], 1))
    whole = jnp.where(zh == 0, by_core, by_core[::-1])
    qa = whole[:, :, 0].reshape(4, 160, 640)
    qg = whole[:, :, 1].reshape(4, 160, 640)
    qg = jnp.stack(
        [lax.dynamic_index_in_dim(qg, quarter ^ r, 0, keepdims=False) for r in range(4)]
    )

    w_send = w_send.astype(BF16)
    w_sum = (w_keep + swap(w_send).astype(F32)).astype(BF16)
    w_send, *operands = lax.optimization_barrier((w_send, *operands))
    fa, fg = pl.pallas_call(
        factor_kernel,
        out_shape=(
            jax.ShapeDtypeStruct((384, 640), F32),
            jax.ShapeDtypeStruct((2, 256, 640), F32),
        ),
        in_specs=[SMEM] + [VMEM] * 10,
        out_specs=(VMEM, VMEM),
        compiler_params=params(),
        cost_estimate=pl.CostEstimate(flops=3 * 10**9, bytes_accessed=10**7, transcendentals=0),
    )(jnp.stack([y, x]).astype(jnp.int32), *operands)
    left = pl.pallas_call(
        left_kernel,
        out_shape=jax.ShapeDtypeStruct((160, 640), BF16),
        in_specs=[VMEM] * 7,
        out_specs=VMEM,
        compiler_params=params(),
        cost_estimate=pl.CostEstimate(flops=10**8, bytes_accessed=3 * 10**6, transcendentals=0),
    )(*sum_over_z(w_sum), qa)

    fa = lax.dynamic_slice_in_dim(fa, (y % 2) * 64, 320, 0).astype(BF16)
    fa = fa.reshape(4, 2, 2, 20, 640).transpose(2, 1, 0, 3, 4).reshape(2, 8, 20, 640)
    fg = lax.dynamic_slice_in_dim(fg, x * 32, 160, 1).astype(BF16)
    fg = fg.reshape(2, 2, 2, 2, 20, 640).transpose(3, 1, 0, 2, 4, 5).reshape(2, 8, 20, 640)
    f_part = jnp.concatenate([fa, fg], axis=2)
    f_part = jnp.stack(
        [
            lax.dynamic_index_in_dim(f_part, lax.rem(z + d, 8), 1, keepdims=False)
            for d in (0, 2, 6, 4, 1, 3, 7, 5)
        ],
        axis=1,
    )
    keep = lax.dynamic_index_in_dim(f_part, core, 0, keepdims=False)
    send = lax.dynamic_index_in_dim(f_part, 1 - core, 0, keepdims=False)
    f_sum = (keep.astype(F32) + swap(send).astype(F32)).astype(BF16)
    factors = sum(p.astype(F32) for p in sum_over_z(f_sum)) / 32768

    pair = [(0, 1), (1, 0), (2, 3), (3, 2)]
    left_far = lax.ppermute(left, "zl", pair)
    lefts = (left, swap(left), left_far, swap(left_far))
    result = pl.pallas_call(
        finish_kernel,
        out_shape=jax.ShapeDtypeStruct((640, 160), BF16),
        in_specs=[VMEM] * 8,
        out_specs=VMEM,
        compiler_params=params(),
        cost_estimate=pl.CostEstimate(flops=10**9, bytes_accessed=3 * 10**6, transcendentals=0),
    )(
        *lefts,
        qg,
        qa,
        lax.dynamic_slice_in_dim(eig_a, block_a, 1, 0),
        lax.dynamic_slice_in_dim(eig_g, block_g, 1, 0).reshape(640, 1),
    )

    moves = []
    for y0 in range(4):
        for l0 in range(4):
            for h0 in range(2):
                y1, l1, h1 = 2 * h0 + y0 // 2, 2 * (y0 % 2) + l0 // 2, l0 % 2
                moves.append(((y0 * 4 + l0) * 2 + h0, (y1 * 4 + l1) * 2 + h1))
    factor_g = lax.ppermute(factors[20:], ("y", "zl", "zh"), moves)
    result = lax.ppermute(result, ("y", "zl", "zh"), moves)
    return factors[:20], factor_g, result[None]


def solution(mesh):
    names = ("x", "y", "zl", "zh", "core")
    fine = Mesh(mesh.devices.reshape(4, 4, 4, 2, 2), names)
    dp, grp = names[:3], names[3:]
    return jax.shard_map(
        body,
        mesh=fine,
        in_specs=(
            P(names, None),
            P(names, None),
            P(None, grp, None),
            P(None, grp, None),
            P(),
            P(),
        ),
        out_specs=(P(names, None), P(names, None), P(dp, None, grp)),
        check_vma=False,
    )
```

```python
import jax
import jax.numpy as jnp
from jax import lax
from jax.experimental import pallas as pl
from jax.experimental.pallas import tpu as pltpu
from jax.sharding import Mesh, PartitionSpec as P

DAMPING = 0.03
ROWS = (((0,), (0,)), ((), ()))
COLS = (((1,), (1,)), ((), ()))
MIB = 1 << 20
F32 = jnp.float32
BF16 = jnp.bfloat16
VMEM = pl.BlockSpec(memory_space=pltpu.VMEM)
SMEM = pl.BlockSpec(memory_space=pltpu.SMEM)
PLACE = (0, 4, 1, 5, 3, 7, 2, 6)
CHIP = (0, 7, 1, 2, 3, 4, 6, 5)
TAKES = tuple(CHIP.index(i) for i in range(8))


def shift(count, by):
    return [(i, (i + by) % count) for i in range(count)]


def z_shift(by):
    at = [(z % 4) * 2 + z // 4 for z in range(8)]
    return [(at[z], at[(z + by) % 8]) for z in range(8)]


def to_z(array, by):
    return lax.ppermute(array, ("zl", "zh"), z_shift(by))


def swap(array, axis="core"):
    return lax.ppermute(array, axis, shift(2, 1))


def params(mib=50):
    return pltpu.CompilerParams(vmem_limit_bytes=mib * MIB)


def exchange(array, axis, count, width):
    me = lax.axis_index(axis)
    pieces = []
    for d in range(count):
        block = lax.dynamic_slice_in_dim(array, lax.rem(me + d, count) * width, width, 1)
        pieces.append(block if d == 0 else lax.ppermute(block, axis, shift(count, d)))
    return jnp.concatenate(pieces, axis=0)


def gather_near(own, axis):
    return own, lax.ppermute(own, axis, shift(4, 1)), lax.ppermute(own, axis, shift(4, 3))


def gather_far(near, axis):
    _, back, ahead = near
    half = back.shape[0] // 2
    return (
        lax.ppermute(back[:half], axis, shift(4, 1)),
        lax.ppermute(ahead[half:], axis, shift(4, 3)),
    )


def rows_of(near, far, d, e, cols):
    if d == 2:
        ref, at = far[e // 2], e % 2
    else:
        ref, at = near[(0, 1, None, 2)[d]], e
    return ref[at * 128 : (at + 1) * 128, cols]


def tokens(near, far, pairs, cols):
    return jnp.concatenate([rows_of(near, far, d, e, cols) for d, e in pairs], axis=0)


def product(left_rows, right_rows, groups):
    total = None
    for group in groups:
        part = lax.dot_general(
            left_rows(group), right_rows(group), ROWS, preferred_element_type=F32
        )
        total = part if total is None else total + part
    return total


def flipped(group):
    return [(e, d) for d, e in group]


NEAR = [[(d, e) for d in (0, 1, 3)] for e in (0, 1, 3)]


def block(i):
    return slice(i * 640, i * 640 + 640)


def near_kernel(*refs):
    acts, grads = refs[:3], refs[3:6]
    total_ref, acts_mid_ref, grads_mid_ref = refs[6:]
    for i in range(3):
        acts_mid_ref[i * 128 : i * 128 + 128] = acts[i][256:384]
        grads_mid_ref[i * 128 : i * 128 + 128] = grads[i][256:384]
    for b in range(2):
        for c in range(2):
            total_ref[b, c] = product(
                lambda g: tokens(grads, None, g, block(c)),
                lambda g: tokens(acts, None, flipped(g), block(b)),
                NEAR,
            )


def far_kernel(where_ref, acts_mid, grads_mid, al, ah, gl, gh, total_ref, keep_ref, send_ref):
    z, core, start = where_ref[0], where_ref[1], where_ref[2]
    for b in range(2):
        for c in range(2):
            bs, cs = block(b), block(c)
            one = lax.dot_general(
                jnp.concatenate([gl[:, cs], gh[128:256, cs]], axis=0),
                acts_mid[:, bs],
                ROWS,
                preferred_element_type=F32,
            )
            two = lax.dot_general(
                jnp.concatenate([grads_mid[:, cs], gh[0:128, cs]], axis=0),
                jnp.concatenate([al[:, bs], ah[128:256, bs], ah[0:128, bs]], axis=0),
                ROWS,
                preferred_element_type=F32,
            )
            total = total_ref[b, c] + one + two
            for q in range(4):
                away = lax.rem(CHIP[4 * b + 2 * c + q // 2] + start - z + 8, 8)
                place = 0
                for d in range(8):
                    place = jnp.where(away == d, PLACE[d], place)
                piece = total[q * 160 : q * 160 + 160].astype(BF16)

                @pl.when(core == q % 2)
                def _():
                    keep_ref[place] = piece

                @pl.when(core != q % 2)
                def _():
                    send_ref[place] = piece


def factor_kernel(where_ref, *refs):
    acts, grads, acts_far, grads_far = refs[:3], refs[3:6], refs[6:8], refs[8:10]
    fa_ref, fg_ref = refs[10:]
    y, x = where_ref[0], where_ref[1]
    groups = [[(d, e) for d in range(4)] for e in range(4)]
    base = pl.multiple_of((y // 2) * 640, 128)
    window = pl.multiple_of((y // 2) * 640 + (y % 2) * 256, 128)
    fa_ref[...] = product(
        lambda g: tokens(acts, acts_far, g, pl.ds(window, 384)),
        lambda g: tokens(acts, acts_far, g, pl.ds(base, 640)),
        groups,
    )
    for c in range(2):
        window = pl.multiple_of(c * 640 + x * 128, 128)
        fg_ref[c] = product(
            lambda g: tokens(grads, grads_far, g, pl.ds(window, 256)),
            lambda g: tokens(grads, grads_far, g, block(c)),
            groups,
        )


def core_sum_kernel(keep, came, here, two, six, to_next, to_prev, up, down):
    def piece(i):
        return (keep[i].astype(F32) + came[i].astype(F32)).astype(BF16)

    here[...] = piece(0)
    two[...] = piece(1)
    six[...] = piece(2)
    opposite = piece(3)
    up[...] = opposite[:80]
    down[...] = opposite[80:]
    for i in range(2):
        to_next[i] = piece(4 + i)
        to_prev[i] = piece(6 + i)


def parity_sum_kernel(two, six, prev, after, up, down, ahead, behind):
    total = two[...].astype(F32) + prev[1].astype(F32)
    ahead[0:80] = (total[:80] + up[...].astype(F32)).astype(BF16)
    ahead[80:160] = total[80:].astype(BF16)
    total = six[...].astype(F32) + after[1].astype(F32)
    behind[0:80] = total[:80].astype(BF16)
    behind[80:160] = (total[80:] + down[...].astype(F32)).astype(BF16)


def left_kernel(here, prev, after, ahead, behind, qa_ref, left_ref):
    total = here[...].astype(F32) + prev[0].astype(F32) + after[0].astype(F32)
    total += ahead[...].astype(F32) + behind[...].astype(F32)
    wgrad = (total / 128).astype(BF16)
    qa = qa_ref[...].reshape(640, 640)
    left_ref[...] = jnp.dot(wgrad, qa, preferred_element_type=F32).astype(BF16)


def finish_kernel(l0, l1, l2, l3, qg_ref, qa_ref, eig_a_ref, eig_g_ref, out_ref):
    rotated = None
    for r, left in enumerate((l0, l1, l2, l3)):
        part = lax.dot_general(qg_ref[r], left[...], ROWS, preferred_element_type=F32)
        rotated = part if rotated is None else rotated + part
    scaled = (rotated / (eig_g_ref[...] * eig_a_ref[...] + DAMPING)).astype(BF16)
    right = jnp.dot(qg_ref[0], scaled, preferred_element_type=F32).astype(BF16)
    out_ref[...] = lax.dot_general(
        qa_ref[...].reshape(640, 640), right, COLS, preferred_element_type=F32
    ).astype(BF16)


def sum_over_z(own):
    prev = to_z(own[4:6], 1)
    after = to_z(own[6:8], 7)
    opposite = to_z(own[3], 4)
    ahead = (own[1].astype(F32) + prev[1].astype(F32)).astype(BF16)
    behind = (own[2].astype(F32) + after[1].astype(F32)).astype(BF16)
    ahead, behind = to_z(ahead, 2), to_z(behind, 6)
    return own[0], prev[0], after[0], opposite, ahead, behind


def call(kernel, out_shapes, operands, flops, moved, scalars=None):
    shapes = [jax.ShapeDtypeStruct(*o) for o in out_shapes]
    out = pl.pallas_call(
        kernel,
        out_shape=shapes,
        in_specs=([] if scalars is None else [SMEM]) + [VMEM] * len(operands),
        out_specs=[VMEM] * len(shapes),
        compiler_params=params(),
        cost_estimate=pl.CostEstimate(flops=flops, bytes_accessed=moved, transcendentals=0),
    )(*([] if scalars is None else [jnp.stack(scalars).astype(jnp.int32)]), *operands)
    return out if len(out) > 1 else out[0]


def body(acts, grads, basis_a, basis_g, eig_a, eig_g):
    x, y, zl, zh, core = (lax.axis_index(n) for n in ("x", "y", "zl", "zh", "core"))
    z = 4 * zh + zl
    start = 2 * (y % 2)

    def takes(chip):
        number = lax.rem(chip - start + 8, 8)
        found = 0
        for i in range(8):
            found = jnp.where(number == i, TAKES[i], found)
        return found

    mine, theirs = takes(z), takes(lax.rem(z + 4, 8))
    block_a, block_g = 2 * x + mine // 4, 2 * y + mine // 2 % 2
    quarter = 2 * (mine % 2) + core

    def basis_pair(piece):
        return jnp.stack(
            [
                lax.dynamic_index_in_dim(basis_a, 2 * x + piece // 4, 0, keepdims=False),
                lax.dynamic_index_in_dim(basis_g, 2 * y + piece // 2 % 2, 0, keepdims=False),
            ]
        )

    basis_far = swap(basis_pair(theirs), "zh")
    acts_x = exchange(acts, "x", 4, 1280)
    grads_y = exchange(grads, "y", 4, 1280)
    acts_near = gather_near(acts_x, "y")
    grads_near = gather_near(grads_y, "x")
    acts_far = gather_far(acts_near, "y")
    grads_far = gather_far(grads_near, "x")

    here = jnp.stack([basis_pair(mine), basis_far])
    sibling = swap(here)
    by_core = jnp.where(core == 0, jnp.stack([here, sibling], 1), jnp.stack([sibling, here], 1))
    whole = jnp.where(zh == 0, by_core, by_core[::-1])
    qa = whole[:, :, 0].reshape(4, 160, 640)
    qg = whole[:, :, 1].reshape(4, 160, 640)
    qg = jnp.stack(
        [lax.dynamic_index_in_dim(qg, quarter ^ r, 0, keepdims=False) for r in range(4)]
    )
    *near, qa, qg = lax.optimization_barrier((*acts_near, *grads_near, qa, qg))

    total, acts_mid, grads_mid = call(
        near_kernel,
        [((2, 2, 640, 640), F32), ((384, 1280), BF16), ((384, 1280), BF16)],
        near,
        4 * 10**9,
        10**7,
    )
    w_keep, w_send = call(
        far_kernel,
        [((8, 160, 640), BF16)] * 2,
        (acts_mid, grads_mid, *acts_far, *grads_far, total),
        3 * 10**9,
        10**7,
        (z, core, start),
    )
    one, both, half = ((160, 640), BF16), ((2, 160, 640), BF16), ((80, 640), BF16)
    own, two, six, to_next, to_prev, up, down = call(
        core_sum_kernel,
        [one, one, one, both, both, half, half],
        (w_keep, swap(w_send)),
        10**6,
        4 * 10**6,
    )
    prev, after = to_z(to_next, 1), to_z(to_prev, 7)
    up, down = to_z(up, 2), to_z(down, 6)
    to_next, *operands = lax.optimization_barrier(
        (to_next, *near, *acts_far, *grads_far)
    )
    fa, fg = call(
        factor_kernel,
        [((384, 640), F32), ((2, 256, 640), F32)],
        operands,
        3 * 10**9,
        10**7,
        (y, x),
    )
    ahead, behind = call(
        parity_sum_kernel, [one, one], (two, six, prev, after, up, down), 10**6, 10**6
    )
    ahead, behind = to_z(ahead, 2), to_z(behind, 6)
    left = call(
        left_kernel, [one], (own, prev, after, ahead, behind, qa), 10**8, 3 * 10**6
    )

    fa = lax.dynamic_slice_in_dim(fa, (y % 2) * 64, 320, 0).astype(BF16)
    fa = fa.reshape(4, 2, 2, 20, 640).transpose(2, 1, 0, 3, 4).reshape(2, 8, 20, 640)
    fg = lax.dynamic_slice_in_dim(fg, x * 32, 160, 1).astype(BF16)
    fg = fg.reshape(2, 2, 2, 2, 20, 640).transpose(3, 1, 0, 2, 4, 5).reshape(2, 8, 20, 640)

    def factor_piece(k):
        pieces = []
        for d in (0, 2, 6, 4, 1, 3, 7, 5):
            chip = lax.rem(z + d, 8)
            rows = [
                lax.dynamic_slice(f, (k, at, 0, 0), (1, 1, 20, 640)).reshape(20, 640)
                for f, at in ((fa, chip), (fg, takes(chip)))
            ]
            pieces.append(jnp.concatenate(rows, axis=0))
        return jnp.stack(pieces)

    f_sum = (factor_piece(core).astype(F32) + swap(factor_piece(1 - core)).astype(F32)).astype(BF16)
    factors = sum(p.astype(F32) for p in sum_over_z(f_sum)) / 32768

    pairs, moves = [], []
    for y0 in range(4):
        for number in range(8):
            b, c, h = number // 4, number // 2 % 2, number % 2
            z0, z1 = ((CHIP[n] + 2 * (y0 % 2)) % 8 for n in (number, number ^ 1))
            at = (y0 * 4 + z0 % 4) * 2 + z0 // 4
            pairs.append((at, (y0 * 4 + z1 % 4) * 2 + z1 // 4))
            moves.append((at, ((2 * b + y0 // 2) * 4 + 2 * (y0 % 2) + c) * 2 + h))
    left_far = lax.ppermute(left, ("y", "zl", "zh"), pairs)
    result = call(
        finish_kernel,
        [((640, 160), BF16)],
        (
            *(left, swap(left), left_far, swap(left_far)),
            qg,
            qa,
            lax.dynamic_slice_in_dim(eig_a, block_a, 1, 0),
            lax.dynamic_slice_in_dim(eig_g, block_g, 1, 0).reshape(640, 1),
        ),
        10**9,
        3 * 10**6,
    )
    factor_g = lax.ppermute(factors[20:], ("y", "zl", "zh"), moves)
    result = lax.ppermute(result, ("y", "zl", "zh"), moves)
    return factors[:20], factor_g, result[None]


def solution(mesh):
    names = ("x", "y", "zl", "zh", "core")
    fine = Mesh(mesh.devices.reshape(4, 4, 4, 2, 2), names)
    dp, grp = names[:3], names[3:]
    return jax.shard_map(
        body,
        mesh=fine,
        in_specs=(
            P(names, None),
            P(names, None),
            P(None, grp, None),
            P(None, grp, None),
            P(),
            P(),
        ),
        out_specs=(P(names, None), P(names, None), P(dp, None, grp)),
        check_vma=False,
    )
```

```python
import jax
import jax.numpy as jnp
from jax import lax
from jax.experimental import pallas as pl
from jax.experimental.pallas import tpu as pltpu
from jax.sharding import Mesh, PartitionSpec as P

DAMPING = 0.03
ROWS = (((0,), (0,)), ((), ()))
COLS = (((1,), (1,)), ((), ()))
MIB = 1 << 20
F32 = jnp.float32
BF16 = jnp.bfloat16
VMEM = pl.BlockSpec(memory_space=pltpu.VMEM)
SMEM = pl.BlockSpec(memory_space=pltpu.SMEM)
PLACE = (0, 4, 1, 5, 3, 7, 2, 6)
CHIP = (0, 7, 1, 2, 3, 4, 6, 5)
DISTANCE = (0, 2, 6, 4, 1, 3, 7, 5)
TAKES = tuple(CHIP.index(i) for i in range(8))


def shift(count, by):
    return [(i, (i + by) % count) for i in range(count)]


def z_shift(by):
    at = [(z % 4) * 2 + z // 4 for z in range(8)]
    return [(at[z], at[(z + by) % 8]) for z in range(8)]


def to_z(array, by):
    return lax.ppermute(array, ("zl", "zh"), z_shift(by))


def swap(array, axis="core"):
    return lax.ppermute(array, axis, shift(2, 1))


def params(mib=24):
    return pltpu.CompilerParams(vmem_limit_bytes=mib * MIB)


def exchange(plans, count, width):
    pieces = [[None] * count for _ in plans]
    for d in (2, 1, 3, 0):
        for (array, axis), got in zip(plans, pieces):
            first = lax.rem(lax.axis_index(axis) + d, count) * width
            cols = lax.dynamic_slice_in_dim(array, first, width, 1)
            got[d] = cols if d == 0 else lax.ppermute(cols, axis, shift(count, d))
    return [jnp.concatenate(got, axis=0) for got in pieces]


def gather_near(own, axis):
    return own, lax.ppermute(own, axis, shift(4, 1)), lax.ppermute(own, axis, shift(4, 3))


def gather_far(near, axis):
    _, back, ahead = near
    half = back.shape[0] // 2
    return (
        lax.ppermute(back[:half], axis, shift(4, 1)),
        lax.ppermute(ahead[half:], axis, shift(4, 3)),
    )


def rows_of(near, outer, inner, cols):
    return near[(0, 1, None, 2)[outer]][inner * 128 : inner * 128 + 128, cols]


def block(i):
    return slice(i * 640, i * 640 + 640)


def product(left, right):
    return lax.dot_general(left, right, ROWS, preferred_element_type=F32)


def factor_rows(where_ref, acts_slab, grads_slab):
    y, x = where_ref[3], where_ref[4]
    base = pl.multiple_of((y // 2) * 640, 128)
    window = pl.multiple_of((y // 2) * 640 + (y % 2) * 256, 128)
    parts = [product(acts_slab(pl.ds(window, 384)), acts_slab(pl.ds(base, 640)))]
    for c in range(2):
        window = pl.multiple_of(c * 640 + x * 128, 128)
        parts.append(product(grads_slab(pl.ds(window, 256)), grads_slab(block(c))))
    return jnp.concatenate(parts, axis=0)


def near_kernel(where_ref, *refs):
    acts, grads = refs[:3], refs[3:6]
    total_ref, factor_ref, acts_mid_ref, grads_mid_ref = refs[6:]
    pairs = [(e, d) for e in (0, 1, 3) for d in (0, 1, 3)]

    def acts_slab(cols):
        return jnp.concatenate([rows_of(acts, e, d, cols) for e, d in pairs], axis=0)

    def grads_slab(cols):
        return jnp.concatenate([rows_of(grads, d, e, cols) for e, d in pairs], axis=0)

    for i, outer in enumerate((0, 1, 3)):
        acts_mid_ref[i * 128 : i * 128 + 128] = rows_of(acts, outer, 2, slice(None))
        grads_mid_ref[i * 128 : i * 128 + 128] = rows_of(grads, outer, 2, slice(None))
    for c in range(2):
        total_ref[c] = product(grads_slab(block(c)), acts_slab(slice(None)))
    factor_ref[...] = factor_rows(where_ref, acts_slab, grads_slab)


def far_kernel(
    where_ref, acts_mid, grads_mid, al, ah, gl, gh, total_ref, factor_ref, order_ref, keep_ref, send_ref
):
    z, core, start = where_ref[0], where_ref[1], where_ref[2]

    def acts_slab(cols):
        return jnp.concatenate(
            [acts_mid[:, cols], al[:, cols], ah[128:256, cols], ah[0:128, cols]], axis=0
        )

    def grads_slab(cols):
        return jnp.concatenate(
            [gl[:, cols], gh[128:256, cols], grads_mid[:, cols], gh[0:128, cols]], axis=0
        )

    for c in range(2):
        total = total_ref[c] + product(grads_slab(block(c)), acts_slab(slice(None)))
        for b in range(2):
            for q in range(4):
                away = lax.rem(CHIP[4 * b + 2 * c + q // 2] + start - z + 8, 8)
                place = 0
                for d in range(8):
                    place = jnp.where(away == d, PLACE[d], place)
                piece = total[q * 160 : q * 160 + 160, block(b)].astype(BF16)

                @pl.when(core == q % 2)
                def _():
                    keep_ref[place, 0:160] = piece

                @pl.when(core != q % 2)
                def _():
                    send_ref[place, 0:160] = piece

    factors = (factor_ref[...] + factor_rows(where_ref, acts_slab, grads_slab)).astype(BF16)
    ordered = jnp.dot(order_ref[...], factors, preferred_element_type=F32).astype(BF16)
    for i in range(8):
        keep_ref[i, 160:208] = ordered[i * 48 : i * 48 + 48]
        send_ref[i, 160:208] = ordered[384 + i * 48 : 384 + i * 48 + 48]


def ordered_rows(x, y, z, core, takes):
    row = jnp.arange(48)
    wanted = []
    for k in (core, 1 - core):
        for d in DISTANCE:
            chip = lax.rem(z + d, 8)
            number = takes(chip)
            of_a = (y % 2) * 64 + 20 * (chip % 4 * 4 + chip // 4 * 2 + k) + row
            of_g = 384 + number // 2 % 2 * 256 + x * 32 + number // 4 * 80
            of_g = of_g + (number % 2 * 2 + k) * 20 + row - 24
            wanted.append(
                jnp.where(row < 20, of_a, jnp.where((row >= 24) & (row < 44), of_g, -1))
            )
    return (jnp.concatenate(wanted)[:, None] == jnp.arange(896)[None, :]).astype(BF16)


def core_sum_kernel(keep, came, here, two, six, to_next, to_prev, up, down):
    def piece(i):
        return (keep[i].astype(F32) + came[i].astype(F32)).astype(BF16)

    here[...] = piece(0)
    two[...] = piece(1)
    six[...] = piece(2)
    opposite = piece(3)
    up[...] = opposite[:96]
    down[...] = opposite[96:]
    for i in range(2):
        to_next[i] = piece(4 + i)
        to_prev[i] = piece(6 + i)


def parity_sum_kernel(two, six, prev, after, up, down, ahead, behind):
    total = two[...].astype(F32) + prev[1].astype(F32)
    ahead[0:96] = (total[:96] + up[...].astype(F32)).astype(BF16)
    ahead[96:208] = total[96:].astype(BF16)
    total = six[...].astype(F32) + after[1].astype(F32)
    behind[0:96] = total[:96].astype(BF16)
    behind[96:208] = (total[96:] + down[...].astype(F32)).astype(BF16)


def left_kernel(here, prev, after, ahead, behind, qa_ref, left_ref, fa_ref, fg_ref):
    total = here[...].astype(F32) + prev[0].astype(F32) + after[0].astype(F32)
    total += ahead[...].astype(F32) + behind[...].astype(F32)
    wgrad = (total[:160] / 128).astype(BF16)
    qa = qa_ref[...].reshape(640, 640)
    left_ref[...] = jnp.dot(wgrad, qa, preferred_element_type=F32).astype(BF16)
    fa_ref[...] = total[160:180] / 32768
    fg_ref[...] = total[184:204] / 32768


def finish_kernel(l0, l1, l2, l3, qg_ref, qa_ref, eig_a_ref, eig_g_ref, out_ref):
    rotated = None
    for r, left in enumerate((l0, l1, l2, l3)):
        part = product(qg_ref[r], left[...])
        rotated = part if rotated is None else rotated + part
    scaled = (rotated / (eig_g_ref[...] * eig_a_ref[...] + DAMPING)).astype(BF16)
    right = jnp.dot(qg_ref[0], scaled, preferred_element_type=F32).astype(BF16)
    qa = qa_ref[...].reshape(640, 640)
    out_ref[...] = lax.dot_general(right, qa, COLS, preferred_element_type=F32).astype(BF16)


def call(kernel, out_shapes, operands, flops, moved, scalars=None):
    shapes = [jax.ShapeDtypeStruct(*o) for o in out_shapes]
    out = pl.pallas_call(
        kernel,
        out_shape=shapes,
        in_specs=([] if scalars is None else [SMEM]) + [VMEM] * len(operands),
        out_specs=[VMEM] * len(shapes),
        compiler_params=params(),
        cost_estimate=pl.CostEstimate(flops=flops, bytes_accessed=moved, transcendentals=0),
    )(*([] if scalars is None else [jnp.stack(scalars).astype(jnp.int32)]), *operands)
    return out if len(out) > 1 else out[0]


def body(acts, grads, basis_a, basis_g, eig_a, eig_g):
    x, y, zl, zh, core = (lax.axis_index(n) for n in ("x", "y", "zl", "zh", "core"))
    z = 4 * zh + zl
    start = 2 * (y % 2)

    def takes(chip):
        number = lax.rem(chip - start + 8, 8)
        found = 0
        for i in range(8):
            found = jnp.where(number == i, TAKES[i], found)
        return found

    mine, theirs = takes(z), takes(lax.rem(z + 4, 8))
    block_a, block_g = 2 * x + mine // 4, 2 * y + mine // 2 % 2
    quarter = 2 * (mine % 2) + core

    def basis_pair(piece):
        return jnp.stack(
            [
                lax.dynamic_index_in_dim(basis_a, 2 * x + piece // 4, 0, keepdims=False),
                lax.dynamic_index_in_dim(basis_g, 2 * y + piece // 2 % 2, 0, keepdims=False),
            ]
        )

    acts_own, grads_own = exchange([(acts, "x"), (grads, "y")], 4, 1280)
    basis_out, acts_own = lax.optimization_barrier((basis_pair(theirs), acts_own))
    basis_far = swap(basis_out, "zh")
    near = (*gather_near(acts_own, "y"), *gather_near(grads_own, "x"))
    acts_far, grads_far = gather_far(near[:3], "y"), gather_far(near[3:], "x")
    order = ordered_rows(x, y, z, core, takes)

    *near, basis_far, order = lax.optimization_barrier((*near, basis_far, order))

    where = (z, core, start, y, x)
    mid = ((384, 1280), BF16)
    total, factor_part, acts_mid, grads_mid = call(
        near_kernel,
        [((2, 640, 1280), F32), ((896, 640), F32), mid, mid],
        near,
        5 * 10**9,
        10**7,
        where,
    )
    w_keep, w_send = call(
        far_kernel,
        [((8, 208, 640), BF16)] * 2,
        (acts_mid, grads_mid, *acts_far, *grads_far, total, factor_part, order),
        4 * 10**9,
        10**7,
        where,
    )
    one, both = ((208, 640), BF16), ((2, 208, 640), BF16)
    own, two, six, to_next, to_prev, up, down = call(
        core_sum_kernel,
        [one, one, one, both, both, ((96, 640), BF16), ((112, 640), BF16)],
        (w_keep, swap(w_send)),
        10**6,
        4 * 10**6,
    )
    basis_far, to_next = lax.optimization_barrier((basis_far, to_next))

    here = jnp.stack([basis_pair(mine), basis_far])
    sibling = swap(here)
    by_core = jnp.where(core == 0, jnp.stack([here, sibling], 1), jnp.stack([sibling, here], 1))
    whole = jnp.where(zh == 0, by_core, by_core[::-1])
    qa = whole[:, :, 0].reshape(4, 160, 640)
    qg = whole[:, :, 1].reshape(4, 160, 640)
    qg = jnp.stack(
        [lax.dynamic_index_in_dim(qg, quarter ^ r, 0, keepdims=False) for r in range(4)]
    )

    prev, after = to_z(to_next, 1), to_z(to_prev, 7)
    up, down = to_z(up, 2), to_z(down, 6)
    ahead, behind = call(
        parity_sum_kernel, [one, one], (two, six, prev, after, up, down), 10**6, 10**6
    )
    ahead, behind = to_z(ahead, 2), to_z(behind, 6)
    left, factor_a, factor_g = call(
        left_kernel,
        [((160, 640), BF16), ((20, 640), F32), ((20, 640), F32)],
        (own, prev, after, ahead, behind, qa),
        10**8,
        3 * 10**6,
    )

    pairs, moves = [], []
    for y0 in range(4):
        for number in range(8):
            b, c, h = number // 4, number // 2 % 2, number % 2
            z0, z1 = ((CHIP[n] + 2 * (y0 % 2)) % 8 for n in (number, number ^ 1))
            at = (y0 * 4 + z0 % 4) * 2 + z0 // 4
            pairs.append((at, (y0 * 4 + z1 % 4) * 2 + z1 // 4))
            moves.append((at, ((2 * b + y0 // 2) * 4 + 2 * (y0 % 2) + c) * 2 + h))
    left_far = lax.ppermute(left, ("y", "zl", "zh"), pairs)
    factor_g = lax.ppermute(factor_g, ("y", "zl", "zh"), moves)
    qg, qa, factor_g = lax.optimization_barrier((qg, qa, factor_g))
    result = call(
        finish_kernel,
        [((160, 640), BF16)],
        (
            *(left, swap(left), left_far, swap(left_far)),
            qg,
            qa,
            lax.dynamic_slice_in_dim(eig_a, block_a, 1, 0),
            lax.dynamic_slice_in_dim(eig_g, block_g, 1, 0).reshape(640, 1),
        ),
        10**9,
        3 * 10**6,
    )
    result = lax.ppermute(result, ("y", "zl", "zh"), moves)
    return factor_a, factor_g, result.T[None]


def solution(mesh):
    names = ("x", "y", "zl", "zh", "core")
    fine = Mesh(mesh.devices.reshape(4, 4, 4, 2, 2), names)
    dp, grp = names[:3], names[3:]
    return jax.shard_map(
        body,
        mesh=fine,
        in_specs=(
            P(names, None),
            P(names, None),
            P(None, grp, None),
            P(None, grp, None),
            P(),
            P(),
        ),
        out_specs=(P(names, None), P(names, None), P(dp, None, grp)),
        check_vma=False,
    )
```

```python
import jax
import jax.numpy as jnp
from jax import lax
from jax.experimental import pallas as pl
from jax.experimental.pallas import tpu as pltpu
from jax.sharding import Mesh, PartitionSpec as P

DAMPING = 0.03
ROWS = (((0,), (0,)), ((), ()))
COLS = (((1,), (1,)), ((), ()))
MIB = 1 << 20
F32 = jnp.float32
BF16 = jnp.bfloat16
VMEM = pl.BlockSpec(memory_space=pltpu.VMEM)
SMEM = pl.BlockSpec(memory_space=pltpu.SMEM)
PLACE = (0, 4, 1, 5, 3, 7, 2, 6)
CHIP = (0, 7, 1, 2, 3, 4, 6, 5)
DISTANCE = (0, 2, 6, 4, 1, 3, 7, 5)
TAKES = tuple(CHIP.index(i) for i in range(8))


def shift(count, by):
    return [(i, (i + by) % count) for i in range(count)]


def z_shift(by):
    at = [(z % 4) * 2 + z // 4 for z in range(8)]
    return [(at[z], at[(z + by) % 8]) for z in range(8)]


def to_z(array, by):
    return lax.ppermute(array, ("zl", "zh"), z_shift(by))


def swap(array, axis="core"):
    return lax.ppermute(array, axis, shift(2, 1))


def params(mib=24):
    return pltpu.CompilerParams(vmem_limit_bytes=mib * MIB)


def exchange(plans, count, width):
    pieces = [[None] * count for _ in plans]
    for d in (2, 1, 3, 0):
        for (array, axis), got in zip(plans, pieces):
            first = lax.rem(lax.axis_index(axis) + d, count) * width
            cols = lax.dynamic_slice_in_dim(array, first, width, 1)
            got[d] = cols if d == 0 else lax.ppermute(cols, axis, shift(count, d))
    return [jnp.concatenate(got, axis=0) for got in pieces]


def gather_near(own, axis):
    return own, lax.ppermute(own, axis, shift(4, 1)), lax.ppermute(own, axis, shift(4, 3))


def gather_far(near, axis):
    _, back, ahead = near
    half = back.shape[0] // 2
    return (
        lax.ppermute(back[:half], axis, shift(4, 1)),
        lax.ppermute(ahead[half:], axis, shift(4, 3)),
    )


def rows_of(near, outer, inner, cols):
    return near[(0, 1, None, 2)[outer]][inner * 128 : inner * 128 + 128, cols]


def block(i):
    return slice(i * 640, i * 640 + 640)


def product(left, right):
    return lax.dot_general(left, right, ROWS, preferred_element_type=F32)


def factor_rows(where_ref, acts_slab, grads_slab):
    y, x = where_ref[3], where_ref[4]
    base = pl.multiple_of((y // 2) * 640, 128)
    window = pl.multiple_of((y // 2) * 640 + (y % 2) * 256, 128)
    parts = [product(acts_slab(pl.ds(window, 384)), acts_slab(pl.ds(base, 640)))]
    for c in range(2):
        window = pl.multiple_of(c * 640 + x * 128, 128)
        parts.append(product(grads_slab(pl.ds(window, 256)), grads_slab(block(c))))
    return jnp.concatenate(parts, axis=0)


def near_kernel(where_ref, *refs):
    acts, grads = refs[:3], refs[3:6]
    total_ref, factor_ref, acts_mid_ref, grads_mid_ref = refs[6:]
    pairs = [(e, d) for e in (0, 1, 3) for d in (0, 1, 3)]

    def acts_slab(cols):
        return jnp.concatenate([rows_of(acts, e, d, cols) for e, d in pairs], axis=0)

    def grads_slab(cols):
        return jnp.concatenate([rows_of(grads, d, e, cols) for e, d in pairs], axis=0)

    for i, outer in enumerate((0, 1, 3)):
        acts_mid_ref[i * 128 : i * 128 + 128] = rows_of(acts, outer, 2, slice(None))
        grads_mid_ref[i * 128 : i * 128 + 128] = rows_of(grads, outer, 2, slice(None))
    for c in range(2):
        total_ref[c] = product(grads_slab(block(c)), acts_slab(slice(None)))
    factor_ref[...] = factor_rows(where_ref, acts_slab, grads_slab)


def far_kernel(
    where_ref, acts_mid, grads_mid, al, ah, gl, gh, total_ref, factor_ref, order_ref, keep_ref, send_ref
):
    z, core, start = where_ref[0], where_ref[1], where_ref[2]

    def acts_slab(cols):
        return jnp.concatenate(
            [acts_mid[:, cols], al[:, cols], ah[128:256, cols], ah[0:128, cols]], axis=0
        )

    def grads_slab(cols):
        return jnp.concatenate(
            [gl[:, cols], gh[128:256, cols], grads_mid[:, cols], gh[0:128, cols]], axis=0
        )

    for c in range(2):
        total = total_ref[c] + product(grads_slab(block(c)), acts_slab(slice(None)))
        for b in range(2):
            for q in range(4):
                away = lax.rem(CHIP[4 * b + 2 * c + q // 2] + start - z + 8, 8)
                place = 0
                for d in range(8):
                    place = jnp.where(away == d, PLACE[d], place)
                piece = total[q * 160 : q * 160 + 160, block(b)].astype(BF16)

                @pl.when(core == q % 2)
                def _():
                    keep_ref[place, 0:160] = piece

                @pl.when(core != q % 2)
                def _():
                    send_ref[place, 0:160] = piece

    factors = (factor_ref[...] + factor_rows(where_ref, acts_slab, grads_slab)).astype(BF16)
    ordered = jnp.dot(order_ref[...], factors, preferred_element_type=F32).astype(BF16)
    for i in range(8):
        keep_ref[i, 160:208] = ordered[i * 48 : i * 48 + 48]
        send_ref[i, 160:208] = ordered[384 + i * 48 : 384 + i * 48 + 48]


def ordered_rows(x, y, z, core, takes):
    row = jnp.arange(48)
    wanted = []
    for k in (core, 1 - core):
        for d in DISTANCE:
            chip = lax.rem(z + d, 8)
            number = takes(chip)
            of_a = (y % 2) * 64 + 20 * (chip % 4 * 4 + chip // 4 * 2 + k) + row
            of_g = 384 + number // 2 % 2 * 256 + x * 32 + number // 4 * 80
            of_g = of_g + (number % 2 * 2 + k) * 20 + row - 24
            wanted.append(
                jnp.where(row < 20, of_a, jnp.where((row >= 24) & (row < 44), of_g, -1))
            )
    return (jnp.concatenate(wanted)[:, None] == jnp.arange(896)[None, :]).astype(BF16)


def core_sum_kernel(keep, came, here, two, six, to_next, to_prev, up, down):
    def piece(i):
        return (keep[i].astype(F32) + came[i].astype(F32)).astype(BF16)

    here[...] = piece(0)
    two[...] = piece(1)
    six[...] = piece(2)
    opposite = piece(3)
    up[...] = opposite[:96]
    down[...] = opposite[96:]
    for i in range(2):
        to_next[i] = piece(4 + i)
        to_prev[i] = piece(6 + i)


def parity_sum_kernel(two, six, prev, after, up, down, ahead, behind):
    total = two[...].astype(F32) + prev[1].astype(F32)
    ahead[0:96] = (total[:96] + up[...].astype(F32)).astype(BF16)
    ahead[96:208] = total[96:].astype(BF16)
    total = six[...].astype(F32) + after[1].astype(F32)
    behind[0:96] = total[:96].astype(BF16)
    behind[96:208] = (total[96:] + down[...].astype(F32)).astype(BF16)


def left_kernel(here, prev, after, ahead, behind, qa_ref, left_ref, fa_ref, fg_ref):
    total = here[...].astype(F32) + prev[0].astype(F32) + after[0].astype(F32)
    total += ahead[...].astype(F32) + behind[...].astype(F32)
    wgrad = (total[:160] / 128).astype(BF16)
    qa = qa_ref[...].reshape(640, 640)
    left_ref[...] = jnp.dot(wgrad, qa, preferred_element_type=F32).astype(BF16)
    fa_ref[...] = total[160:180] / 32768
    fg_ref[...] = total[184:204] / 32768


def finish_kernel(l0, l1, l2, l3, qg_ref, qa_ref, eig_a_ref, eig_g_ref, out_ref):
    rotated = None
    for r, left in enumerate((l0, l1, l2, l3)):
        part = product(qg_ref[r], left[...])
        rotated = part if rotated is None else rotated + part
    scaled = (rotated / (eig_g_ref[...] * eig_a_ref[...] + DAMPING)).astype(BF16)
    right = jnp.dot(qg_ref[0], scaled, preferred_element_type=F32).astype(BF16)
    qa = qa_ref[...].reshape(640, 640)
    out_ref[...] = lax.dot_general(right, qa, COLS, preferred_element_type=F32).astype(BF16)


def call(kernel, out_shapes, operands, flops, moved, scalars=None):
    shapes = [jax.ShapeDtypeStruct(*o) for o in out_shapes]
    out = pl.pallas_call(
        kernel,
        out_shape=shapes,
        in_specs=([] if scalars is None else [SMEM]) + [VMEM] * len(operands),
        out_specs=[VMEM] * len(shapes),
        compiler_params=params(),
        cost_estimate=pl.CostEstimate(flops=flops, bytes_accessed=moved, transcendentals=0),
    )(*([] if scalars is None else [jnp.stack(scalars).astype(jnp.int32)]), *operands)
    return out if len(out) > 1 else out[0]


def body(acts, grads, basis_a, basis_g, eig_a, eig_g):
    x, y, zl, zh, core = (lax.axis_index(n) for n in ("x", "y", "zl", "zh", "core"))
    z = 4 * zh + zl
    start = 2 * (y % 2)

    def takes(chip):
        number = lax.rem(chip - start + 8, 8)
        found = 0
        for i in range(8):
            found = jnp.where(number == i, TAKES[i], found)
        return found

    mine, theirs = takes(z), takes(lax.rem(z + 4, 8))
    block_a, block_g = 2 * x + mine // 4, 2 * y + mine // 2 % 2
    quarter = 2 * (mine % 2) + core

    def basis_pair(piece):
        return jnp.stack(
            [
                lax.dynamic_index_in_dim(basis_a, 2 * x + piece // 4, 0, keepdims=False),
                lax.dynamic_index_in_dim(basis_g, 2 * y + piece // 2 % 2, 0, keepdims=False),
            ]
        )

    acts_own, grads_own = exchange([(acts, "x"), (grads, "y")], 4, 1280)
    basis_out, basis_mine, acts_own = lax.optimization_barrier(
        (basis_pair(theirs), basis_pair(mine), acts_own)
    )
    basis_far = swap(basis_out, "zh")
    near = (*gather_near(acts_own, "y"), *gather_near(grads_own, "x"))
    acts_far, grads_far = gather_far(near[:3], "y"), gather_far(near[3:], "x")
    order = ordered_rows(x, y, z, core, takes)

    *near, basis_far, order = lax.optimization_barrier((*near, basis_far, order))

    where = (z, core, start, y, x)
    mid = ((384, 1280), BF16)
    total, factor_part, acts_mid, grads_mid = call(
        near_kernel,
        [((2, 640, 1280), F32), ((896, 640), F32), mid, mid],
        near,
        5 * 10**9,
        10**7,
        where,
    )
    w_keep, w_send = call(
        far_kernel,
        [((8, 208, 640), BF16)] * 2,
        (acts_mid, grads_mid, *acts_far, *grads_far, total, factor_part, order),
        4 * 10**9,
        10**7,
        where,
    )
    one, both = ((208, 640), BF16), ((2, 208, 640), BF16)
    own, two, six, to_next, to_prev, up, down = call(
        core_sum_kernel,
        [one, one, one, both, both, ((96, 640), BF16), ((112, 640), BF16)],
        (w_keep, swap(w_send)),
        10**6,
        4 * 10**6,
    )
    prev, after = to_z(to_next, 1), to_z(to_prev, 7)
    up, down = to_z(up, 2), to_z(down, 6)
    ahead, behind = call(
        parity_sum_kernel, [one, one], (two, six, prev, after, up, down), 10**6, 10**6
    )
    ahead, basis_mine, basis_far = lax.optimization_barrier((ahead, basis_mine, basis_far))
    ahead, behind = to_z(ahead, 2), to_z(behind, 6)

    def by_core(rows):
        other = swap(rows)
        return jnp.where(core == 0, jnp.stack([rows, other], 1), jnp.stack([other, rows], 1))

    near_rows, far_rows = by_core(basis_mine), by_core(basis_far)
    whole = jnp.where(
        zh == 0,
        jnp.concatenate([near_rows, far_rows], axis=1),
        jnp.concatenate([far_rows, near_rows], axis=1),
    )
    qa = whole[0]
    qg = jnp.stack(
        [lax.dynamic_index_in_dim(whole[1], quarter ^ r, 0, keepdims=False) for r in range(4)]
    )
    left, factor_a, factor_g = call(
        left_kernel,
        [((160, 640), BF16), ((20, 640), F32), ((20, 640), F32)],
        (own, prev, after, ahead, behind, qa),
        10**8,
        3 * 10**6,
    )

    pairs, moves = [], []
    for y0 in range(4):
        for number in range(8):
            b, c, h = number // 4, number // 2 % 2, number % 2
            z0, z1 = ((CHIP[n] + 2 * (y0 % 2)) % 8 for n in (number, number ^ 1))
            at = (y0 * 4 + z0 % 4) * 2 + z0 // 4
            pairs.append((at, (y0 * 4 + z1 % 4) * 2 + z1 // 4))
            moves.append((at, ((2 * b + y0 // 2) * 4 + 2 * (y0 % 2) + c) * 2 + h))
    left_far = lax.ppermute(left, ("y", "zl", "zh"), pairs)
    factor_g = lax.ppermute(factor_g, ("y", "zl", "zh"), moves)
    qg, qa, factor_g = lax.optimization_barrier((qg, qa, factor_g))
    result = call(
        finish_kernel,
        [((160, 640), BF16)],
        (
            *(left, swap(left), left_far, swap(left_far)),
            qg,
            qa,
            lax.dynamic_slice_in_dim(eig_a, block_a, 1, 0),
            lax.dynamic_slice_in_dim(eig_g, block_g, 1, 0).reshape(640, 1),
        ),
        10**9,
        3 * 10**6,
    )
    result = lax.ppermute(result, ("y", "zl", "zh"), moves)
    return factor_a, factor_g, result.T[None]


def solution(mesh):
    names = ("x", "y", "zl", "zh", "core")
    fine = Mesh(mesh.devices.reshape(4, 4, 4, 2, 2), names)
    dp, grp = names[:3], names[3:]
    return jax.shard_map(
        body,
        mesh=fine,
        in_specs=(
            P(names, None),
            P(names, None),
            P(None, grp, None),
            P(None, grp, None),
            P(),
            P(),
        ),
        out_specs=(P(names, None), P(names, None), P(dp, None, grp)),
        check_vma=False,
    )
```

```python
import jax
import jax.numpy as jnp
from jax import lax
from jax.experimental import pallas as pl
from jax.experimental.pallas import tpu as pltpu
from jax.sharding import Mesh, PartitionSpec as P

DAMPING = 0.03
ROWS = (((0,), (0,)), ((), ()))
COLS = (((1,), (1,)), ((), ()))
MIB = 1 << 20
F32 = jnp.float32
BF16 = jnp.bfloat16
VMEM = pl.BlockSpec(memory_space=pltpu.VMEM)
SMEM = pl.BlockSpec(memory_space=pltpu.SMEM)
PLACE = (0, 4, 1, 5, 3, 7, 2, 6)
CHIP = (0, 7, 1, 2, 3, 4, 6, 5)
DISTANCE = (0, 2, 6, 4, 1, 3, 7, 5)
TAKES = tuple(CHIP.index(i) for i in range(8))


def shift(count, by):
    return [(i, (i + by) % count) for i in range(count)]


def z_shift(by):
    at = [(z % 4) * 2 + z // 4 for z in range(8)]
    return [(at[z], at[(z + by) % 8]) for z in range(8)]


def to_z(array, by):
    return lax.ppermute(array, ("zl", "zh"), z_shift(by))


def swap(array, axis="core"):
    return lax.ppermute(array, axis, shift(2, 1))


def params(mib=24):
    return pltpu.CompilerParams(vmem_limit_bytes=mib * MIB)


def exchange(plans, count, width):
    pieces = [[None] * count for _ in plans]
    for d in (2, 1, 3, 0):
        for (array, axis), got in zip(plans, pieces):
            first = lax.rem(lax.axis_index(axis) + d, count) * width
            cols = lax.dynamic_slice_in_dim(array, first, width, 1)
            got[d] = cols if d == 0 else lax.ppermute(cols, axis, shift(count, d))
    return [jnp.concatenate(got, axis=0) for got in pieces]


def gather_near(own, axis):
    return own, lax.ppermute(own, axis, shift(4, 1)), lax.ppermute(own, axis, shift(4, 3))


def gather_far(near, axis):
    _, back, ahead = near
    half = back.shape[0] // 2
    return (
        lax.ppermute(back[:half], axis, shift(4, 1)),
        lax.ppermute(ahead[half:], axis, shift(4, 3)),
    )


def rows_of(near, outer, inner, cols):
    return near[(0, 1, None, 2)[outer]][inner * 128 : inner * 128 + 128, cols]


def block(i):
    return slice(i * 640, i * 640 + 640)


def product(left, right):
    return lax.dot_general(left, right, ROWS, preferred_element_type=F32)


def factor_rows(where_ref, acts_slab, grads_slab):
    y, x = where_ref[3], where_ref[4]
    base = pl.multiple_of((y // 2) * 640, 128)
    window = pl.multiple_of((y // 2) * 640 + (y % 2) * 256, 128)
    parts = [product(acts_slab(pl.ds(window, 384)), acts_slab(pl.ds(base, 640)))]
    for c in range(2):
        window = pl.multiple_of(c * 640 + x * 128, 128)
        parts.append(product(grads_slab(pl.ds(window, 256)), grads_slab(block(c))))
    return jnp.concatenate(parts, axis=0)


def near_kernel(where_ref, *refs):
    acts, grads = refs[:3], refs[3:6]
    total_ref, factor_ref, acts_mid_ref, grads_mid_ref = refs[6:]
    pairs = [(e, d) for e in (0, 1, 3) for d in (0, 1, 3)]

    def acts_slab(cols):
        return jnp.concatenate([rows_of(acts, e, d, cols) for e, d in pairs], axis=0)

    def grads_slab(cols):
        return jnp.concatenate([rows_of(grads, d, e, cols) for e, d in pairs], axis=0)

    for i, outer in enumerate((0, 1, 3)):
        acts_mid_ref[i * 128 : i * 128 + 128] = rows_of(acts, outer, 2, slice(None))
        grads_mid_ref[i * 128 : i * 128 + 128] = rows_of(grads, outer, 2, slice(None))
    for c in range(2):
        total_ref[c] = product(grads_slab(block(c)), acts_slab(slice(None)))
    factor_ref[...] = factor_rows(where_ref, acts_slab, grads_slab)


def far_kernel(
    where_ref, acts_mid, grads_mid, al, ah, gl, gh, total_ref, factor_ref, order_ref, keep_ref, send_ref
):
    z, core, start = where_ref[0], where_ref[1], where_ref[2]

    def acts_slab(cols):
        return jnp.concatenate(
            [acts_mid[:, cols], al[:, cols], ah[128:256, cols], ah[0:128, cols]], axis=0
        )

    def grads_slab(cols):
        return jnp.concatenate(
            [gl[:, cols], gh[128:256, cols], grads_mid[:, cols], gh[0:128, cols]], axis=0
        )

    for c in range(2):
        total = total_ref[c] + product(grads_slab(block(c)), acts_slab(slice(None)))
        for b in range(2):
            for q in range(4):
                away = lax.rem(CHIP[4 * b + 2 * c + q // 2] + start - z + 8, 8)
                place = 0
                for d in range(8):
                    place = jnp.where(away == d, PLACE[d], place)
                piece = total[q * 160 : q * 160 + 160, block(b)].astype(BF16)

                @pl.when(core == q % 2)
                def _():
                    keep_ref[place, 0:160] = piece

                @pl.when(core != q % 2)
                def _():
                    send_ref[place, 0:160] = piece

    factors = (factor_ref[...] + factor_rows(where_ref, acts_slab, grads_slab)).astype(BF16)
    ordered = jnp.dot(order_ref[...], factors, preferred_element_type=F32).astype(BF16)
    for i in range(8):
        keep_ref[i, 160:208] = ordered[i * 48 : i * 48 + 48]
        send_ref[i, 160:208] = ordered[384 + i * 48 : 384 + i * 48 + 48]


def ordered_rows(x, y, z, core, takes):
    row = jnp.arange(48)
    wanted = []
    for k in (core, 1 - core):
        for d in DISTANCE:
            chip = lax.rem(z + d, 8)
            number = takes(chip)
            of_a = (y % 2) * 64 + 20 * (chip % 4 * 4 + chip // 4 * 2 + k) + row
            of_g = 384 + number // 2 % 2 * 256 + x * 32 + number // 4 * 80
            of_g = of_g + (number % 2 * 2 + k) * 20 + row - 24
            wanted.append(
                jnp.where(row < 20, of_a, jnp.where((row >= 24) & (row < 44), of_g, -1))
            )
    return (jnp.concatenate(wanted)[:, None] == jnp.arange(896)[None, :]).astype(BF16)


def core_sum_kernel(keep, came, here, two, six, to_next, to_prev, up, down):
    def piece(i):
        return (keep[i].astype(F32) + came[i].astype(F32)).astype(BF16)

    here[...] = piece(0)
    two[...] = piece(1)
    six[...] = piece(2)
    opposite = piece(3)
    up[...] = opposite[:96]
    down[...] = opposite[96:]
    for i in range(2):
        to_next[i] = piece(4 + i)
        to_prev[i] = piece(6 + i)


def parity_sum_kernel(two, six, prev, after, up, down, ahead, behind):
    total = two[...].astype(F32) + prev[1].astype(F32)
    ahead[0:96] = (total[:96] + up[...].astype(F32)).astype(BF16)
    ahead[96:208] = total[96:].astype(BF16)
    total = six[...].astype(F32) + after[1].astype(F32)
    behind[0:96] = total[:96].astype(BF16)
    behind[96:208] = (total[96:] + down[...].astype(F32)).astype(BF16)


def left_kernel(here, prev, after, ahead, behind, qa_ref, left_ref, fa_ref, fg_ref):
    total = here[...].astype(F32) + prev[0].astype(F32) + after[0].astype(F32)
    total += ahead[...].astype(F32) + behind[...].astype(F32)
    wgrad = (total[:160] / 128).astype(BF16)
    qa = qa_ref[...].reshape(640, 640)
    left_ref[...] = jnp.dot(wgrad, qa, preferred_element_type=F32).astype(BF16)
    fa_ref[...] = total[160:180] / 32768
    fg_ref[...] = total[184:204] / 32768


def finish_kernel(l0, l1, l2, l3, qg_ref, qa_ref, eig_a_ref, eig_g_ref, out_ref):
    rotated = None
    for r, left in enumerate((l0, l1, l2, l3)):
        part = product(qg_ref[r], left[...])
        rotated = part if rotated is None else rotated + part
    scaled = (rotated / (eig_g_ref[...] * eig_a_ref[...] + DAMPING)).astype(BF16)
    right = jnp.dot(qg_ref[0], scaled, preferred_element_type=F32).astype(BF16)
    qa = qa_ref[...].reshape(640, 640)
    out_ref[...] = lax.dot_general(right, qa, COLS, preferred_element_type=F32).astype(BF16)


def call(kernel, out_shapes, operands, flops, moved, scalars=None):
    shapes = [jax.ShapeDtypeStruct(*o) for o in out_shapes]
    out = pl.pallas_call(
        kernel,
        out_shape=shapes,
        in_specs=([] if scalars is None else [SMEM]) + [VMEM] * len(operands),
        out_specs=[VMEM] * len(shapes),
        compiler_params=params(),
        cost_estimate=pl.CostEstimate(flops=flops, bytes_accessed=moved, transcendentals=0),
    )(*([] if scalars is None else [jnp.stack(scalars).astype(jnp.int32)]), *operands)
    return out if len(out) > 1 else out[0]


def body(acts, grads, basis_a, basis_g, eig_a, eig_g):
    x, y, zl, zh, core = (lax.axis_index(n) for n in ("x", "y", "zl", "zh", "core"))
    z = 4 * zh + zl
    start = 2 * (y % 2)

    def takes(chip):
        number = lax.rem(chip - start + 8, 8)
        found = 0
        for i in range(8):
            found = jnp.where(number == i, TAKES[i], found)
        return found

    mine, theirs = takes(z), takes(lax.rem(z + 4, 8))
    block_a, block_g = 2 * x + mine // 4, 2 * y + mine // 2 % 2
    quarter = 2 * (mine % 2) + core

    def basis_pair(piece):
        return jnp.stack(
            [
                lax.dynamic_index_in_dim(basis_a, 2 * x + piece // 4, 0, keepdims=False),
                lax.dynamic_index_in_dim(basis_g, 2 * y + piece // 2 % 2, 0, keepdims=False),
            ]
        )

    acts_own, grads_own = exchange([(acts, "x"), (grads, "y")], 4, 1280)
    basis_out, basis_mine, acts_own = lax.optimization_barrier(
        (basis_pair(theirs), basis_pair(mine), acts_own)
    )
    basis_far = swap(basis_out, "zh")
    near = (*gather_near(acts_own, "y"), *gather_near(grads_own, "x"))
    acts_far, grads_far = gather_far(near[:3], "y"), gather_far(near[3:], "x")
    order = ordered_rows(x, y, z, core, takes)

    *near, basis_far, order = lax.optimization_barrier((*near, basis_far, order))

    where = (z, core, start, y, x)
    mid = ((384, 1280), BF16)
    total, factor_part, acts_mid, grads_mid = call(
        near_kernel,
        [((2, 640, 1280), F32), ((896, 640), F32), mid, mid],
        near,
        5 * 10**9,
        10**7,
        where,
    )
    w_keep, w_send = call(
        far_kernel,
        [((8, 208, 640), BF16)] * 2,
        (acts_mid, grads_mid, *acts_far, *grads_far, total, factor_part, order),
        4 * 10**9,
        10**7,
        where,
    )
    one, both = ((208, 640), BF16), ((2, 208, 640), BF16)
    own, two, six, to_next, to_prev, up, down = call(
        core_sum_kernel,
        [one, one, one, both, both, ((96, 640), BF16), ((112, 640), BF16)],
        (w_keep, swap(w_send)),
        10**6,
        4 * 10**6,
    )
    prev, after = to_z(to_next, 1), to_z(to_prev, 7)
    up, down = to_z(up, 2), to_z(down, 6)
    ahead, behind = call(
        parity_sum_kernel, [one, one], (two, six, prev, after, up, down), 10**6, 10**6
    )
    ahead, basis_mine, basis_far = lax.optimization_barrier((ahead, basis_mine, basis_far))
    ahead, behind = to_z(ahead, 2), to_z(behind, 6)

    def by_core(rows):
        other = swap(rows)
        return jnp.where(core == 0, jnp.stack([rows, other], 1), jnp.stack([other, rows], 1))

    near_rows, far_rows = by_core(basis_mine), by_core(basis_far)
    whole = jnp.where(
        zh == 0,
        jnp.concatenate([near_rows, far_rows], axis=1),
        jnp.concatenate([far_rows, near_rows], axis=1),
    )
    qa = whole[0]
    qg = jnp.stack(
        [lax.dynamic_index_in_dim(whole[1], quarter ^ r, 0, keepdims=False) for r in range(4)]
    )
    left, factor_a, factor_g = call(
        left_kernel,
        [((160, 640), BF16), ((20, 640), F32), ((20, 640), F32)],
        (own, prev, after, ahead, behind, qa),
        10**8,
        3 * 10**6,
    )

    pairs, moves = [], []
    for y0 in range(4):
        for number in range(8):
            b, c, h = number // 4, number // 2 % 2, number % 2
            z0, z1 = ((CHIP[n] + 2 * (y0 % 2)) % 8 for n in (number, number ^ 1))
            at = (y0 * 4 + z0 % 4) * 2 + z0 // 4
            pairs.append((at, (y0 * 4 + z1 % 4) * 2 + z1 // 4))
            moves.append((at, ((2 * b + y0 // 2) * 4 + 2 * (y0 % 2) + c) * 2 + h))
    left_far = lax.ppermute(left, ("y", "zl", "zh"), pairs)
    factor_g = lax.ppermute(factor_g, ("y", "zl", "zh"), moves)
    result = call(
        finish_kernel,
        [((160, 640), BF16)],
        (
            *(left, swap(left), left_far, swap(left_far)),
            qg,
            qa,
            lax.dynamic_slice_in_dim(eig_a, block_a, 1, 0),
            lax.dynamic_slice_in_dim(eig_g, block_g, 1, 0).reshape(640, 1),
        ),
        10**9,
        3 * 10**6,
    )
    result, factor_g = lax.optimization_barrier((result, factor_g))
    result = lax.ppermute(result, ("y", "zl", "zh"), moves)
    return factor_a, factor_g, result.T[None]


def solution(mesh):
    names = ("x", "y", "zl", "zh", "core")
    fine = Mesh(mesh.devices.reshape(4, 4, 4, 2, 2), names)
    dp, grp = names[:3], names[3:]
    return jax.shard_map(
        body,
        mesh=fine,
        in_specs=(
            P(names, None),
            P(names, None),
            P(None, grp, None),
            P(None, grp, None),
            P(),
            P(),
        ),
        out_specs=(P(names, None), P(names, None), P(dp, None, grp)),
        check_vma=False,
    )
```
